32 devices in a mesh: groups: 2 (over y), row: 4 (over x, core), col: 4 (over z).
Axes of the slice: x: 2, y: 2, z: 4, core: 2. Of those that a mesh axis runs over, the one named last changes fastest.
Arguments:
- pair_rep: float32 [256, 128, 128], P(('groups', 'row'), 'col'), parts along dimension 0, may hold values from -6 to 6
- chain_ids: int32 [256], P('groups'), parts along dimension 0, may hold values from 0 to 5, never falling along the last dimension, each value on 1 to 64 neighbouring positions
- residue_mask: int32 [256], P('groups'), parts along dimension 0, may hold values from 0 to 1, as said below
- norm_gain: float32 [128], replicated, may hold values from 0.1 to 1.9
- norm_bias: float32 [128], replicated, may hold values from -3 to 3
- chain_bias: float32 [128], replicated, may hold values from -4 to 4
- proj_in: bfloat16 [128, 640], replicated, may hold values from -0.5 to 0.5
- out_gain: float32 [128], replicated, may hold values from 0.1 to 1.9
- out_bias: float32 [128], replicated, may hold values from -3 to 3
- proj_out: bfloat16 [128, 128], replicated, may hold values from -0.5 to 0.5
Outputs:
- pair_next: float32 [256, 128, 128], P(('groups', 'row'), 'col'), parts along dimension 0
The draws below stay inside these ranges and needn't reach their ends.
There are 2 independent parts, one for each index of `groups`. The reference program is written for one: setup_inputs(seed, part) draws one part's arguments, and reference() takes and returns one part's arrays. A program takes and returns all parts, laid end to end along the dimension named above; an argument that names none is the same for every part. Nothing has to cross between parts.
Inputs may be any that keep to these rules, and one draw needn't show every extreme that they name: `chain_ids`: chain numbers never decrease along the residues, and every chain number appears. `residue_mask`: the residues below a length of at least 64 and below 128 are 1, all later ones 0.
All inputs are finite; a program needn't handle non-finite values.
Results may differ from the reference program's by a relative error of at most 0.0021.
Values may be sent and summed in bfloat16 or wider, within the bound.
A program may use at most 128 MiB of HBM per device.

```python
import math
import jax
import jax.numpy as jnp
import numpy as np
from jax import lax

C = 128
TOKENS = 128


def draw_residue_mask(key, part):
    key = jax.random.fold_in(key, 7)
    length = jax.random.randint(key, (), TOKENS // 2, TOKENS)
    return (jnp.arange(TOKENS) < length).astype(jnp.int32)


def level_of(stream_key, extent, cuts, smallest, high):
    level, own = 1.0, jax.random.fold_in(stream_key, 6)
    for position, blocks in cuts:
        draws = jnp.exp(jax.random.uniform(jax.random.fold_in(own, position), (blocks,), jnp.float32, smallest / len(cuts), high / len(cuts)))
        level = level * jnp.repeat(draws, extent[position] // blocks).reshape([-1 if axis == position else 1 for axis in range(len(extent))])
    return level


def profile(number_of, total, limit, skew):
    portions = [(1 << 20) // math.isqrt(rank ** skew) + 1 for rank in range(2, number_of + 1)]
    rest, counts = total - limit - (number_of - 1), [1] * (number_of - 1)
    while rest > 0:
        candidates = [i for i in range(number_of - 1) if counts[i] < limit]
        pool, budget = sum([portions[i] for i in candidates]), rest
        for i in candidates:
            extra = min(limit - counts[i], max(1, budget * portions[i] // pool), rest)
            counts[i] = counts[i] + extra
            rest = rest - extra
    return np.array([limit] + counts)


def uneven_parts(key, number_of, total, reach, lean):
    if number_of == 2:
        one = jax.random.randint(key, (), max(1, total - reach), min(reach, total - 1) + 1)
        return jnp.stack([one, total - one])
    lengths = jnp.asarray(profile(number_of, total, reach, lean), jnp.int32)
    pairs = (number_of - 1) // 2
    source_of, sink = lengths[1:1 + 2 * pairs:2], lengths[2:2 + 2 * pairs:2]
    margin = jnp.minimum(source_of - 1, reach - sink)
    moved = jax.random.randint(jax.random.fold_in(key, 1), (pairs,), 0, 1 << 20) % (margin + 1)
    lengths = lengths.at[1:1 + 2 * pairs:2].set(source_of - moved).at[2:2 + 2 * pairs:2].set(sink + moved)
    return lengths[jax.random.permutation(jax.random.fold_in(key, 2), number_of)]


def normal_values(key, extent, width, bound, shards=(), dtype=jnp.bfloat16):
    factor_of = level_of(key, extent, shards, -0.22, 0.18) if shards else 1.0
    entries = jax.random.normal(key, extent, jnp.float32) * width * factor_of
    return jnp.minimum(jnp.maximum(entries, -bound), bound).astype(dtype)


def setup_inputs(seed: int = 0, part: int = 0) -> dict:
    seeds = jax.random.split(jax.random.key(seed), 11)
    own_keys = jax.random.split(jax.random.fold_in(seeds[10], part), 11)
    pair_rep = normal_values(own_keys[0], (TOKENS, TOKENS, C), 1.0, 6.0, ((0, 4), (1, 4)), jnp.float32)
    chain_ids = jnp.searchsorted(jnp.cumsum(uneven_parts(own_keys[1], 6, TOKENS, TOKENS // 2, 1)), jnp.arange(TOKENS), side="right").astype(jnp.int32)
    residue_mask = draw_residue_mask(jax.random.fold_in(jax.random.fold_in(seeds[10], part), 71), part)
    norm_gain = jnp.clip(1.0 + 0.18 * jax.random.normal(seeds[3], (C,), jnp.float32), 0.1, 1.9)
    norm_bias = normal_values(seeds[4], (C,), 0.5, 3.0, (), jnp.float32)
    chain_bias = normal_values(seeds[5], (C,), 1.0, 4.0, (), jnp.float32)
    proj_in = normal_values(seeds[6], (C, 5 * C), C ** -0.5, 0.5)
    out_gain = jnp.clip(1.0 + 0.18 * jax.random.normal(seeds[7], (C,), jnp.float32), 0.1, 1.9)
    out_bias = normal_values(seeds[8], (C,), 0.5, 3.0, (), jnp.float32)
    proj_out = normal_values(seeds[9], (C, C), C ** -0.5, 0.5)
    return dict(pair_rep=pair_rep, chain_ids=chain_ids, residue_mask=residue_mask, norm_gain=norm_gain, norm_bias=norm_bias, chain_bias=chain_bias, proj_in=proj_in, out_gain=out_gain, out_bias=out_bias, proj_out=proj_out)


def layer_norm(values, gain, bias):
    center = values - lax.optimization_barrier(jnp.mean(values, axis=-1, keepdims=True))
    variance = lax.optimization_barrier(jnp.mean(center * center, axis=-1, keepdims=True))
    return center * lax.rsqrt(variance + 1e-05) * gain + bias

def reference(pair_rep, chain_ids, residue_mask, norm_gain, norm_bias, chain_bias, proj_in, out_gain, out_bias, proj_out):
    same_chain = (chain_ids[:, None] == chain_ids[None, :]).astype(jnp.float32)
    pair_in = pair_rep + same_chain[:, :, None] * chain_bias
    normed = layer_norm(pair_in, norm_gain, norm_bias).astype(jnp.bfloat16)
    projected = jnp.dot(normed.reshape(-1, C), proj_in, preferred_element_type=jnp.float32)
    projected = projected.reshape(TOKENS, TOKENS, 5 * C)
    live_res = residue_mask.astype(jnp.float32)
    pair_mask = (live_res[:, None] * live_res[None, :])[:, :, None]
    left = (jax.nn.sigmoid(projected[:, :, 0:C]) * projected[:, :, C:2 * C] * pair_mask).astype(jnp.bfloat16)
    right = (jax.nn.sigmoid(projected[:, :, 2 * C:3 * C]) * projected[:, :, 3 * C:4 * C] * pair_mask).astype(jnp.bfloat16)
    gate_vals = jax.nn.sigmoid(projected[:, :, 4 * C:5 * C])
    mixed = jnp.einsum('ikc,jkc->ijc', left.astype(jnp.float32), right.astype(jnp.float32), precision=lax.Precision.HIGHEST)
    mixed_norm = layer_norm(mixed, out_gain, out_bias).astype(jnp.bfloat16)
    update = jnp.dot(mixed_norm.reshape(-1, C), proj_out, preferred_element_type=jnp.float32)
    return pair_rep + gate_vals * update.reshape(TOKENS, TOKENS, C)
```

```python
import functools

import jax
import jax.numpy as jnp
from jax import lax
from jax.experimental import pallas as pl
from jax.experimental.pallas import tpu as pltpu
from jax.sharding import PartitionSpec as P

C = 128
G = 8
J = 16
F32 = jnp.float32
BF16 = jnp.bfloat16


def layer_norm(values, gain, bias):
    center = values - jnp.mean(values, axis=-1, keepdims=True)
    variance = jnp.mean(center * center, axis=-1, keepdims=True)
    return center * lax.rsqrt(variance + 1e-05) * gain + bias


def as_rows(ref, offset, count):
    shape = (count, ref.shape[1])
    lane = lax.broadcasted_iota(jnp.int32, shape, 1)
    row = lax.broadcasted_iota(jnp.int32, shape, 0)
    values = jnp.broadcast_to(ref[...].astype(F32), shape)
    picked = jnp.sum(jnp.where(lane == row + offset, values, 0.0), axis=1, keepdims=True)
    return jnp.broadcast_to(picked, (count, C))


def kernel(
    R,
    N,
    pair_ref,
    chain_ref,
    mask_ref,
    gain_ref,
    bias_ref,
    chain_bias_ref,
    w_in_ref,
    out_gain_ref,
    out_bias_ref,
    w_out_ref,
    out_ref,
    row_chain,
    col_chain,
    row_live,
    col_live,
    normed,
    left,
    right,
    right_k,
    rights,
    own,
    outbox,
    inbox,
    direct_send,
    core_send,
    right_recv,
    sum_send,
    sum_recv,
):
    rows, cols, _ = pair_ref.shape
    chunks = rows // J
    parts = cols // J
    r = lax.axis_index("row")
    c = lax.axis_index("col")
    sibling = r + 1 - 2 * lax.rem(r, 2)
    half = R // 2

    barrier = pltpu.get_barrier_semaphore()
    pl.semaphore_signal(barrier, inc=1, device_id={"row": sibling})
    for d in range(1, half):
        pl.semaphore_signal(barrier, inc=1, device_id={"row": lax.rem(r + 2 * d, R)})
    for d in range(1, N):
        pl.semaphore_signal(barrier, inc=1, device_id={"col": lax.rem(c + d, N)})

    row_chain[...] = as_rows(chain_ref, r * rows, rows)
    col_chain[...] = as_rows(chain_ref, c * cols, cols)
    row_live[...] = as_rows(mask_ref, r * rows, rows)
    col_live[...] = as_rows(mask_ref, c * cols, cols)

    def direct_copy(d, q):
        return pltpu.make_async_remote_copy(
            src_ref=rights.at[r, q],
            dst_ref=rights.at[r, q],
            send_sem=direct_send.at[d, q],
            recv_sem=right_recv.at[r, q],
            device_id={"row": lax.rem(r + 2 * d, R)},
        )

    def core_copy(d, q):
        source = lax.rem(r + R - 2 * d, R)
        return pltpu.make_async_remote_copy(
            src_ref=rights.at[source, q],
            dst_ref=rights.at[source, q],
            send_sem=core_send.at[d, q],
            recv_sem=right_recv.at[source, q],
            device_id={"row": sibling},
        )

    def right_arrival(source, q):
        return pltpu.make_async_remote_copy(
            src_ref=rights.at[source, q],
            dst_ref=rights.at[source, q],
            send_sem=core_send.at[0, q],
            recv_sem=right_recv.at[source, q],
            device_id={"row": sibling},
        )

    def sum_copy(dest, p):
        return pltpu.make_async_remote_copy(
            src_ref=outbox.at[dest, p],
            dst_ref=inbox.at[c, p],
            send_sem=sum_send.at[dest, p],
            recv_sem=sum_recv.at[c, p],
            device_id={"col": dest},
        )

    def sum_arrival(source, p):
        return pltpu.make_async_remote_copy(
            src_ref=outbox.at[source, p],
            dst_ref=inbox.at[source, p],
            send_sem=sum_send.at[source, p],
            recv_sem=sum_recv.at[source, p],
            device_id={"col": source},
        )

    def gated(base, columns, target, rounded):
        tokens = pl.ds(pl.multiple_of(base * cols, G * cols), G * cols)
        product = jnp.dot(normed[tokens, :], w_in_ref[:, columns], preferred_element_type=F32)
        for i in range(G):
            block = product[i * cols : (i + 1) * cols]
            mask = row_live[pl.ds(base + i, 1), :] * col_live[...]
            value = jax.nn.sigmoid(block[:, :C]) * block[:, C:] * mask
            if rounded:
                value = value.astype(BF16).astype(F32)
            target[pl.ds(pl.multiple_of((base + i) * cols, cols), cols), :] = value

    def right_group(g, carry):
        base = g * G
        for i in range(G):
            same = row_chain[pl.ds(base + i, 1), :] == col_chain[...]
            pair_in = pair_ref[base + i] + jnp.where(same, chain_bias_ref[...], 0.0)
            tokens = pl.ds(pl.multiple_of((base + i) * cols, cols), cols)
            normed[tokens, :] = layer_norm(pair_in, gain_ref[...], bias_ref[...]).astype(BF16)
        gated(base, slice(2 * C, 4 * C), right, False)
        return carry

    for q in range(chunks):
        lax.fori_loop(q * (J // G), (q + 1) * (J // G), right_group, 0)
        for k in range(cols):
            rights[r, q, k] = right[pl.ds(q * J * cols + k, J, stride=cols), :].astype(BF16)
        if q == 0:
            pl.semaphore_wait(barrier, 1 + (half - 1) + (N - 1))
        for d in range(1, half):
            direct_copy(d, q).start()
        core_copy(0, q).start()

    def left_group(g, carry):
        gated(g * G, slice(0, 2 * C), left, True)
        return carry

    lax.fori_loop(0, rows // G, left_group, 0)

    def block(source, q):
        start = source * rows + q * J
        dest = start // cols
        p = lax.rem(start, cols) // J
        for k in range(cols):
            right_k[k] = rights[source, q, k].astype(F32)

        def group(g, carry):
            totals = [jnp.zeros((J, C), F32)] * G
            for k in range(cols):
                factor = right_k[k]
                for i in range(G):
                    totals[i] += left[pl.ds((g * G + i) * cols + k, 1), :] * factor

            @pl.when(dest == c)
            def _():
                for i in range(G):
                    own[p, g * G + i] = totals[i]

            @pl.when(dest != c)
            def _():
                for i in range(G):
                    outbox[dest, p, g * G + i] = totals[i].astype(BF16)

            return carry

        lax.fori_loop(0, rows // G, group, 0)

        @pl.when(dest != c)
        def _():
            sum_copy(dest, p).start()

    for d in range(half):
        source = lax.rem(r + R - 2 * d, R)
        other = lax.rem(sibling + R - 2 * d, R)

        def mine(q, carry):
            if d > 0:
                right_arrival(source, q).wait_recv()
                core_copy(d, q).start()
            block(source, q)
            return carry

        def siblings(q, carry):
            right_arrival(other, q).wait_recv()
            block(other, q)
            return carry

        lax.fori_loop(0, chunks, mine, 0)
        lax.fori_loop(0, chunks, siblings, 0)

    def gate_group(g, carry):
        tokens = pl.ds(pl.multiple_of(g * G * cols, G * cols), G * cols)
        product = jnp.dot(normed[tokens, :], w_in_ref[:, 4 * C :], preferred_element_type=F32)
        out_ref[pl.ds(g * G, G)] = jax.nn.sigmoid(product).reshape(G, cols, C)
        return carry

    lax.fori_loop(0, rows // G, gate_group, 0)

    for p in range(parts):
        for d in range(1, N):
            sum_arrival(lax.rem(c + d, N), p).wait_recv()

        def final_group(g, carry):
            group = pl.ds(g * G, G)
            mixed = own[p, group]
            for d in range(1, N):
                mixed += inbox[lax.rem(c + d, N), p, group].astype(F32)
            mixed_norm = layer_norm(mixed.reshape(G * J, C), out_gain_ref[...], out_bias_ref[...])
            update = jnp.dot(mixed_norm.astype(BF16), w_out_ref[...], preferred_element_type=F32)
            where = (group, pl.ds(p * J, J))
            out_ref[where] = out_ref[where] * update.reshape(G, J, C)
            return carry

        lax.fori_loop(0, rows // G, final_group, 0)

    for q in range(chunks):
        for d in range(half):
            if d > 0:
                direct_copy(d, q).wait_send()
            core_copy(d, q).wait_send()
    for d in range(1, N):
        for p in range(parts):
            sum_copy(lax.rem(c + d, N), p).wait_send()


def solution(mesh):
    R, N = mesh.shape["row"], mesh.shape["col"]

    def per_device(
        pair_rep,
        chain_ids,
        residue_mask,
        norm_gain,
        norm_bias,
        chain_bias,
        proj_in,
        out_gain,
        out_bias,
        proj_out,
    ):
        rows, cols, _ = pair_rep.shape
        chunks, parts = rows // J, cols // J
        tokens = rows * cols
        dma = pltpu.SemaphoreType.DMA
        update = pl.pallas_call(
            functools.partial(kernel, R, N),
            out_shape=jax.ShapeDtypeStruct(pair_rep.shape, F32),
            in_specs=[pl.BlockSpec(memory_space=pltpu.VMEM)] * 10,
            out_specs=pl.BlockSpec(memory_space=pltpu.VMEM),
            scratch_shapes=[
                pltpu.VMEM((rows, C), F32),
                pltpu.VMEM((cols, C), F32),
                pltpu.VMEM((rows, C), F32),
                pltpu.VMEM((cols, C), F32),
                pltpu.VMEM((tokens, C), BF16),
                pltpu.VMEM((tokens, C), F32),
                pltpu.VMEM((tokens, C), F32),
                pltpu.VMEM((cols, J, C), F32),
                pltpu.VMEM((R, chunks, cols, J, C), BF16),
                pltpu.VMEM((parts, rows, J, C), F32),
                pltpu.VMEM((N, parts, rows, J, C), BF16),
                pltpu.VMEM((N, parts, rows, J, C), BF16),
                dma((R // 2, chunks)),
                dma((R // 2, chunks)),
                dma((R, chunks)),
                dma((N, parts)),
                dma((N, parts)),
            ],
            compiler_params=pltpu.CompilerParams(
                collective_id=0, has_side_effects=True, vmem_limit_bytes=48 * 1024 * 1024
            ),
        )(
            pair_rep,
            chain_ids.reshape(1, -1),
            residue_mask.reshape(1, -1),
            norm_gain.reshape(1, C),
            norm_bias.reshape(1, C),
            chain_bias.reshape(1, C),
            proj_in,
            out_gain.reshape(1, C),
            out_bias.reshape(1, C),
            proj_out,
        )
        return pair_rep + update

    return jax.shard_map(
        per_device,
        mesh=mesh,
        in_specs=(
            P(("groups", "row"), "col", None),
            P("groups"),
            P("groups"),
            P(),
            P(),
            P(),
            P(),
            P(),
            P(),
            P(),
        ),
        out_specs=P(("groups", "row"), "col", None),
        check_vma=False,
    )
```

```python
import functools
import math

import jax
import jax.numpy as jnp
from jax import lax
from jax.experimental import pallas as pl
from jax.experimental.pallas import tpu as pltpu
from jax.sharding import PartitionSpec as P

C = 128
G = 8
J = 16
F32 = jnp.float32
BF16 = jnp.bfloat16


def layer_norm(values, gain, bias):
    center = values - jnp.mean(values, axis=-1, keepdims=True)
    variance = jnp.mean(center * center, axis=-1, keepdims=True)
    return center * lax.rsqrt(variance + 1e-05) * gain + bias


def as_rows(ref, offset, count):
    shape = (count, ref.shape[1])
    lane = lax.broadcasted_iota(jnp.int32, shape, 1)
    row = lax.broadcasted_iota(jnp.int32, shape, 0)
    values = jnp.broadcast_to(ref[...].astype(F32), shape)
    picked = jnp.sum(jnp.where(lane == row + offset, values, 0.0), axis=1, keepdims=True)
    return jnp.broadcast_to(picked, (count, C))


def kernel(
    R,
    N,
    pair_hbm,
    chain_hbm,
    mask_hbm,
    gain_hbm,
    bias_hbm,
    chain_bias_hbm,
    w_in_hbm,
    out_gain_hbm,
    out_bias_hbm,
    w_out_hbm,
    out_ref,
    pair_ref,
    chain_ref,
    mask_ref,
    gain_ref,
    bias_ref,
    chain_bias_ref,
    w_in_ref,
    out_gain_ref,
    out_bias_ref,
    w_out_ref,
    row_chain,
    col_chain,
    row_live,
    col_live,
    normed,
    left,
    right,
    right_k,
    rights,
    kept,
    outbox,
    inbox,
    load_sem,
    pair_sem,
    direct_send,
    core_send,
    right_recv,
    sum_send,
    sum_recv,
    pass_recv,
):
    rows, cols, _ = pair_ref.shape
    chunks = rows // J
    parts = cols // J
    r = lax.axis_index("row")
    c = lax.axis_index("col")
    sibling = r + 1 - 2 * lax.rem(r, 2)
    half = R // 2

    smalls = [
        (chain_hbm, chain_ref),
        (mask_hbm, mask_ref),
        (gain_hbm, gain_ref),
        (bias_hbm, bias_ref),
        (chain_bias_hbm, chain_bias_ref),
        (w_in_hbm, w_in_ref),
        (out_gain_hbm, out_gain_ref),
        (out_bias_hbm, out_bias_ref),
        (w_out_hbm, w_out_ref),
    ]
    loads = [
        pltpu.make_async_copy(src, dst, load_sem.at[n]) for n, (src, dst) in enumerate(smalls)
    ]
    pair_loads = [
        pltpu.make_async_copy(
            pair_hbm.at[pl.ds(q * J, J)], pair_ref.at[pl.ds(q * J, J)], pair_sem.at[q]
        )
        for q in range(chunks)
    ]
    for load in loads[:2] + pair_loads[:1] + loads[2:] + pair_loads[1:]:
        load.start()

    barrier = pltpu.get_barrier_semaphore()
    pl.semaphore_signal(barrier, inc=1, device_id={"row": sibling})
    for d in range(1, half):
        pl.semaphore_signal(barrier, inc=1, device_id={"row": lax.rem(r + 2 * d, R)})
    for d in range(1, N):
        pl.semaphore_signal(barrier, inc=1, device_id={"col": lax.rem(c + d, N)})

    for load in loads[:2]:
        load.wait()
    row_chain[...] = as_rows(chain_ref, r * rows, rows)
    col_chain[...] = as_rows(chain_ref, c * cols, cols)
    row_live[...] = as_rows(mask_ref, r * rows, rows)
    col_live[...] = as_rows(mask_ref, c * cols, cols)

    def direct_copy(d, q):
        return pltpu.make_async_remote_copy(
            src_ref=rights.at[r, q],
            dst_ref=rights.at[r, q],
            send_sem=direct_send.at[d, q],
            recv_sem=right_recv.at[r, q],
            device_id={"row": lax.rem(r + 2 * d, R)},
        )

    def core_copy(d, q):
        source = lax.rem(r + R - 2 * d, R)
        return pltpu.make_async_remote_copy(
            src_ref=rights.at[source, q],
            dst_ref=rights.at[source, q],
            send_sem=core_send.at[d, q],
            recv_sem=right_recv.at[source, q],
            device_id={"row": sibling},
        )

    def right_arrival(source, q):
        return pltpu.make_async_remote_copy(
            src_ref=rights.at[source, q],
            dst_ref=rights.at[source, q],
            send_sem=core_send.at[0, q],
            recv_sem=right_recv.at[source, q],
            device_id={"row": sibling},
        )

    def passes_on(device, dest):
        if N < 4:
            return False
        low = jnp.logical_and(device == 0, dest >= 2)
        return jnp.logical_or(low, jnp.logical_and(device == N - 1, dest <= N - 3))

    def adds_to(device, dest):
        if N < 4:
            return False
        low = jnp.logical_and(device == 1, dest >= 2)
        return jnp.logical_or(low, jnp.logical_and(device == N - 2, dest <= N - 3))

    inner = jnp.where(c == 0, 1, N - 2)
    outer = jnp.where(c == 1, 0, N - 1)

    def pass_copy(dest, p):
        return pltpu.make_async_remote_copy(
            src_ref=outbox.at[dest, p],
            dst_ref=outbox.at[dest, p],
            send_sem=sum_send.at[dest, p],
            recv_sem=pass_recv.at[dest, p],
            device_id={"col": inner},
        )

    def pass_arrival(dest, p):
        return pltpu.make_async_remote_copy(
            src_ref=outbox.at[dest, p],
            dst_ref=outbox.at[dest, p],
            send_sem=sum_send.at[dest, p],
            recv_sem=pass_recv.at[dest, p],
            device_id={"col": outer},
        )

    def sum_copy(dest, p):
        return pltpu.make_async_remote_copy(
            src_ref=outbox.at[dest, p],
            dst_ref=inbox.at[c, p],
            send_sem=sum_send.at[dest, p],
            recv_sem=sum_recv.at[c, p],
            device_id={"col": dest},
        )

    def sum_arrival(source, p):
        return pltpu.make_async_remote_copy(
            src_ref=outbox.at[source, p],
            dst_ref=inbox.at[source, p],
            send_sem=sum_send.at[source, p],
            recv_sem=sum_recv.at[source, p],
            device_id={"col": source},
        )

    def gated(base, columns, target, rounded):
        tokens = pl.ds(pl.multiple_of(base * cols, G * cols), G * cols)
        product = jnp.dot(normed[tokens, :], w_in_ref[:, columns], preferred_element_type=F32)
        for i in range(G):
            block = product[i * cols : (i + 1) * cols]
            mask = row_live[pl.ds(base + i, 1), :] * col_live[...]
            value = jax.nn.sigmoid(block[:, :C]) * block[:, C:] * mask
            if rounded:
                value = value.astype(BF16).astype(F32)
            target[pl.ds(pl.multiple_of((base + i) * cols, cols), cols), :] = value

    def right_group(base):
        for i in range(J):
            same = row_chain[pl.ds(base + i, 1), :] == col_chain[...]
            pair_in = pair_ref[base + i] + jnp.where(same, chain_bias_ref[...], 0.0)
            tokens = pl.ds(pl.multiple_of((base + i) * cols, cols), cols)
            normed[tokens, :] = layer_norm(pair_in, gain_ref[...], bias_ref[...]).astype(BF16)
        for g in range(J // G):
            gated(base + g * G, slice(2 * C, 4 * C), right, False)

    for q in range(chunks):
        if q == 0:
            for load in loads[2:6]:
                load.wait()
        pair_loads[q].wait()
        right_group(q * J)
        for k in range(cols):
            rights[r, q, k] = right[pl.ds(q * J * cols + k, J, stride=cols), :].astype(BF16)
        if q == 0:
            pl.semaphore_wait(barrier, 1 + (half - 1) + (N - 1))
        for d in range(1, half):
            direct_copy(d, q).start()
        core_copy(0, q).start()

    def left_group(q, carry):
        for g in range(J // G):
            gated(q * J + g * G, slice(0, 2 * C), left, True)
        return carry

    lax.fori_loop(0, chunks, left_group, 0)

    def dest_of(source, q):
        start = source * rows + q * J
        return start // cols, lax.rem(start, cols) // J

    def block(source, q):
        dest, p = dest_of(source, q)
        keep = jnp.logical_or(dest == c, adds_to(c, dest))
        for k in range(cols):
            right_k[k] = rights[source, q, k].astype(F32)

        def group(g, carry):
            totals = [jnp.zeros((J, C), F32)] * G
            for k in range(cols):
                factor = right_k[k]
                for i in range(G):
                    totals[i] += left[pl.ds((g * G + i) * cols + k, 1), :] * factor

            @pl.when(keep)
            def _():
                for i in range(G):
                    kept[dest, p, g * G + i] = totals[i]

            @pl.when(jnp.logical_not(keep))
            def _():
                for i in range(G):
                    outbox[dest, p, g * G + i] = totals[i].astype(BF16)

            return carry

        lax.fori_loop(0, rows // G, group, 0)

        @pl.when(jnp.logical_not(keep))
        def _():
            if N < 4:
                sum_copy(dest, p).start()
            else:

                @pl.when(passes_on(c, dest))
                def _():
                    pass_copy(dest, p).start()

                @pl.when(jnp.logical_not(passes_on(c, dest)))
                def _():
                    sum_copy(dest, p).start()

    def forward(source, q):
        dest, p = dest_of(source, q)

        @pl.when(adds_to(c, dest))
        def _():
            pass_arrival(dest, p).wait_recv()

            def group(g, carry):
                where = (dest, p, pl.ds(g * G, G))
                outbox[where] = (kept[where] + outbox[where].astype(F32)).astype(BF16)
                return carry

            lax.fori_loop(0, rows // G, group, 0)
            sum_copy(dest, p).start()

    for d in range(half):
        source = lax.rem(r + R - 2 * d, R)
        other = lax.rem(sibling + R - 2 * d, R)

        def mine(q, carry):
            if d > 0:
                right_arrival(source, q).wait_recv()
                core_copy(d, q).start()
            block(source, q)
            return carry

        def siblings(q, carry):
            right_arrival(other, q).wait_recv()
            block(other, q)
            return carry

        lax.fori_loop(0, chunks, mine, 0)
        lax.fori_loop(0, chunks, siblings, 0)

    if N >= 4:
        for d in range(half):
            for source in (lax.rem(r + R - 2 * d, R), lax.rem(sibling + R - 2 * d, R)):

                def passed(q, carry):
                    forward(source, q)
                    return carry

                lax.fori_loop(0, chunks, passed, 0)

    def gate_group(g, carry):
        tokens = pl.ds(pl.multiple_of(g * G * cols, G * cols), G * cols)
        product = jnp.dot(normed[tokens, :], w_in_ref[:, 4 * C :], preferred_element_type=F32)
        out_ref[pl.ds(g * G, G)] = jax.nn.sigmoid(product).reshape(G, cols, C)
        return carry

    lax.fori_loop(0, rows // G, gate_group, 0)

    for load in loads[6:]:
        load.wait()

    if N < 4:
        sources = [lax.rem(c + d, N) for d in range(1, N)]
    else:
        ends = jnp.where(c == 1, 0, jnp.where(c == N - 2, N - 1, c))
        sources = [jnp.where(c == n, ends, n) for n in range(1, N - 1)]

    for p in range(parts):
        for source in sources:
            if N <= 4:
                sum_arrival(source, p).wait_recv()
            else:

                @pl.when(source != c)
                def _():
                    sum_arrival(source, p).wait_recv()

                    def collect(g, carry):
                        group = pl.ds(g * G, G)
                        kept[c, p, group] += inbox[source, p, group].astype(F32)
                        return carry

                    lax.fori_loop(0, rows // G, collect, 0)

        def final_group(g, carry):
            group = pl.ds(g * J, J)
            mixed = kept[c, p, group]
            if N <= 4:
                for source in sources:
                    mixed += inbox[source, p, group].astype(F32)
            mixed_norm = layer_norm(mixed.reshape(J * J, C), out_gain_ref[...], out_bias_ref[...])
            update = jnp.dot(mixed_norm.astype(BF16), w_out_ref[...], preferred_element_type=F32)
            where = (group, pl.ds(p * J, J))
            out_ref[where] = out_ref[where] * update.reshape(J, J, C)
            return carry

        lax.fori_loop(0, chunks, final_group, 0)

    for q in range(chunks):
        for d in range(half):
            if d > 0:
                direct_copy(d, q).wait_send()
            core_copy(d, q).wait_send()
    for d in range(1, N):
        for p in range(parts):
            sum_copy(lax.rem(c + d, N), p).wait_send()


def solution(mesh):
    R, N = mesh.shape["row"], mesh.shape["col"]

    def per_device(
        pair_rep,
        chain_ids,
        residue_mask,
        norm_gain,
        norm_bias,
        chain_bias,
        proj_in,
        out_gain,
        out_bias,
        proj_out,
    ):
        rows, cols, _ = pair_rep.shape
        chunks, parts = rows // J, cols // J
        tokens = rows * cols
        dma = pltpu.SemaphoreType.DMA
        buffers = [
            pltpu.VMEM(pair_rep.shape, F32),
            pltpu.VMEM((1, chain_ids.shape[0]), jnp.int32),
            pltpu.VMEM((1, chain_ids.shape[0]), jnp.int32),
            pltpu.VMEM((1, C), F32),
            pltpu.VMEM((1, C), F32),
            pltpu.VMEM((1, C), F32),
            pltpu.VMEM(proj_in.shape, BF16),
            pltpu.VMEM((1, C), F32),
            pltpu.VMEM((1, C), F32),
            pltpu.VMEM(proj_out.shape, BF16),
            pltpu.VMEM((rows, C), F32),
            pltpu.VMEM((cols, C), F32),
            pltpu.VMEM((rows, C), F32),
            pltpu.VMEM((cols, C), F32),
            pltpu.VMEM((tokens, C), BF16),
            pltpu.VMEM((tokens, C), F32),
            pltpu.VMEM((tokens, C), F32),
            pltpu.VMEM((cols, J, C), F32),
            pltpu.VMEM((R, chunks, cols, J, C), BF16),
            pltpu.VMEM((N, parts, rows, J, C), F32),
            pltpu.VMEM((N, parts, rows, J, C), BF16),
            pltpu.VMEM((N, parts, rows, J, C), BF16),
        ]
        semaphores = [
            dma((9,)),
            dma((chunks,)),
            dma((R // 2, chunks)),
            dma((R // 2, chunks)),
            dma((R, chunks)),
            dma((N, parts)),
            dma((N, parts)),
            dma((N, parts)),
        ]
        held = sum(math.prod(b.shape) * jnp.dtype(b.dtype).itemsize for b in buffers)
        update = pl.pallas_call(
            functools.partial(kernel, R, N),
            out_shape=jax.ShapeDtypeStruct(pair_rep.shape, F32),
            in_specs=[pl.BlockSpec(memory_space=pltpu.HBM)] * 10,
            out_specs=pl.BlockSpec(memory_space=pltpu.VMEM),
            scratch_shapes=buffers + semaphores,
            compiler_params=pltpu.CompilerParams(
                collective_id=0, has_side_effects=True, vmem_limit_bytes=held + 8 * 1024 * 1024
            ),
        )(
            pair_rep,
            chain_ids.reshape(1, -1),
            residue_mask.reshape(1, -1),
            norm_gain.reshape(1, C),
            norm_bias.reshape(1, C),
            chain_bias.reshape(1, C),
            proj_in,
            out_gain.reshape(1, C),
            out_bias.reshape(1, C),
            proj_out,
        )
        return pair_rep + update

    return jax.shard_map(
        per_device,
        mesh=mesh,
        in_specs=(
            P(("groups", "row"), "col", None),
            P("groups"),
            P("groups"),
            P(),
            P(),
            P(),
            P(),
            P(),
            P(),
            P(),
        ),
        out_specs=P(("groups", "row"), "col", None),
        check_vma=False,
    )
```

```python
import functools
import math

import jax
import jax.numpy as jnp
from jax import lax
from jax.experimental import pallas as pl
from jax.experimental.pallas import tpu as pltpu
from jax.sharding import PartitionSpec as P

C = 128
G = 8
J = 16
DEPTH = 2
F32 = jnp.float32
BF16 = jnp.bfloat16


def layer_norm(values, gain, bias):
    center = values - jnp.mean(values, axis=-1, keepdims=True)
    variance = jnp.mean(center * center, axis=-1, keepdims=True)
    return center * lax.rsqrt(variance + 1e-05) * gain + bias


def as_rows(ref, offset, count):
    shape = (count, ref.shape[1])
    lane = lax.broadcasted_iota(jnp.int32, shape, 1)
    row = lax.broadcasted_iota(jnp.int32, shape, 0)
    values = jnp.broadcast_to(ref[...].astype(F32), shape)
    picked = jnp.sum(jnp.where(lane == row + offset, values, 0.0), axis=1, keepdims=True)
    return jnp.broadcast_to(picked, (count, C))


def kernel(
    R,
    N,
    pair_hbm,
    chain_hbm,
    mask_hbm,
    gain_hbm,
    bias_hbm,
    chain_bias_hbm,
    w_in_hbm,
    out_gain_hbm,
    out_bias_hbm,
    w_out_hbm,
    out_ref,
    pair_ref,
    chain_ref,
    mask_ref,
    gain_ref,
    bias_ref,
    chain_bias_ref,
    w_in_ref,
    out_gain_ref,
    out_bias_ref,
    w_out_ref,
    row_chain,
    col_chain,
    row_live,
    col_live,
    normed,
    left,
    right,
    right_k,
    rights,
    kept,
    outbox,
    inbox,
    load_sem,
    pair_sem,
    direct_send,
    core_send,
    right_recv,
    sum_send,
    sum_recv,
    pass_recv,
    end_send,
):
    rows, cols, _ = pair_ref.shape
    chunks = rows // J
    parts = cols // J
    r = lax.axis_index("row")
    c = lax.axis_index("col")
    sibling = r + 1 - 2 * lax.rem(r, 2)
    half = R // 2

    smalls = [
        (chain_hbm, chain_ref),
        (mask_hbm, mask_ref),
        (gain_hbm, gain_ref),
        (bias_hbm, bias_ref),
        (chain_bias_hbm, chain_bias_ref),
        (w_in_hbm, w_in_ref),
        (out_gain_hbm, out_gain_ref),
        (out_bias_hbm, out_bias_ref),
        (w_out_hbm, w_out_ref),
    ]
    loads = [
        pltpu.make_async_copy(src, dst, load_sem.at[n]) for n, (src, dst) in enumerate(smalls)
    ]
    pair_loads = [
        pltpu.make_async_copy(
            pair_hbm.at[pl.ds(q * J, J)], pair_ref.at[pl.ds(q * J, J)], pair_sem.at[q]
        )
        for q in range(chunks)
    ]
    for load in loads[:2] + pair_loads[:1] + loads[2:] + pair_loads[1:]:
        load.start()

    barrier = pltpu.get_barrier_semaphore()
    pl.semaphore_signal(barrier, inc=1, device_id={"row": sibling})
    for d in range(1, half):
        pl.semaphore_signal(barrier, inc=1, device_id={"row": lax.rem(r + 2 * d, R)})
    for d in range(1, N):
        pl.semaphore_signal(barrier, inc=1, device_id={"col": lax.rem(c + d, N)})

    for load in loads[:2]:
        load.wait()
    row_chain[...] = as_rows(chain_ref, r * rows, rows)
    col_chain[...] = as_rows(chain_ref, c * cols, cols)
    row_live[...] = as_rows(mask_ref, r * rows, rows)
    col_live[...] = as_rows(mask_ref, c * cols, cols)

    def direct_copy(d, q):
        return pltpu.make_async_remote_copy(
            src_ref=rights.at[r, q],
            dst_ref=rights.at[r, q],
            send_sem=direct_send.at[d, q],
            recv_sem=right_recv.at[r, q],
            device_id={"row": lax.rem(r + 2 * d, R)},
        )

    def core_copy(d, q):
        source = lax.rem(r + R - 2 * d, R)
        return pltpu.make_async_remote_copy(
            src_ref=rights.at[source, q],
            dst_ref=rights.at[source, q],
            send_sem=core_send.at[d, q],
            recv_sem=right_recv.at[source, q],
            device_id={"row": sibling},
        )

    def right_arrival(source, q):
        return pltpu.make_async_remote_copy(
            src_ref=rights.at[source, q],
            dst_ref=rights.at[source, q],
            send_sem=core_send.at[0, q],
            recv_sem=right_recv.at[source, q],
            device_id={"row": sibling},
        )

    def passes_on(device, dest):
        if N < 4:
            return False
        low = jnp.logical_and(device == 0, dest >= 2)
        return jnp.logical_or(low, jnp.logical_and(device == N - 1, dest <= N - 3))

    def adds_to(device, dest):
        if N < 4:
            return False
        low = jnp.logical_and(device == 1, dest >= 2)
        return jnp.logical_or(low, jnp.logical_and(device == N - 2, dest <= N - 3))

    inner = jnp.where(c == 0, 1, N - 2)
    outer = jnp.where(c == 1, 0, N - 1)

    def pass_copy(dest, p, send_sem):
        return pltpu.make_async_remote_copy(
            src_ref=outbox.at[dest, p],
            dst_ref=outbox.at[dest, p],
            send_sem=send_sem,
            recv_sem=pass_recv.at[dest, p],
            device_id={"col": inner},
        )

    def pass_arrival(dest, p):
        return pltpu.make_async_remote_copy(
            src_ref=outbox.at[dest, p],
            dst_ref=outbox.at[dest, p],
            send_sem=sum_send.at[dest, p],
            recv_sem=pass_recv.at[dest, p],
            device_id={"col": outer},
        )

    def sum_copy(dest, p, send_sem=None):
        return pltpu.make_async_remote_copy(
            src_ref=outbox.at[dest, p],
            dst_ref=inbox.at[c, p],
            send_sem=sum_send.at[dest, p] if send_sem is None else send_sem,
            recv_sem=sum_recv.at[c, p],
            device_id={"col": dest},
        )

    def sum_arrival(source, p):
        return pltpu.make_async_remote_copy(
            src_ref=outbox.at[source, p],
            dst_ref=inbox.at[source, p],
            send_sem=sum_send.at[source, p],
            recv_sem=sum_recv.at[source, p],
            device_id={"col": source},
        )

    def gated(base, columns, target, rounded):
        tokens = pl.ds(pl.multiple_of(base * cols, G * cols), G * cols)
        product = jnp.dot(normed[tokens, :], w_in_ref[:, columns], preferred_element_type=F32)
        for i in range(G):
            block = product[i * cols : (i + 1) * cols]
            mask = row_live[pl.ds(base + i, 1), :] * col_live[...]
            value = jax.nn.sigmoid(block[:, :C]) * block[:, C:] * mask
            if rounded:
                value = value.astype(BF16).astype(F32)
            target[pl.ds(pl.multiple_of((base + i) * cols, cols), cols), :] = value

    def right_group(base):
        for i in range(J):
            same = row_chain[pl.ds(base + i, 1), :] == col_chain[...]
            pair_in = pair_ref[base + i] + jnp.where(same, chain_bias_ref[...], 0.0)
            tokens = pl.ds(pl.multiple_of((base + i) * cols, cols), cols)
            normed[tokens, :] = layer_norm(pair_in, gain_ref[...], bias_ref[...]).astype(BF16)
        for g in range(J // G):
            gated(base + g * G, slice(2 * C, 4 * C), right, False)

    for q in range(chunks):
        if q == 0:
            for load in loads[2:6]:
                load.wait()
        pair_loads[q].wait()
        right_group(q * J)
        for k in range(cols):
            rights[r, q, k] = right[pl.ds(q * J * cols + k, J, stride=cols), :].astype(BF16)
        if q == 0:
            pl.semaphore_wait(barrier, 1 + (half - 1) + (N - 1))
        for d in range(1, half):
            direct_copy(d, q).start()
        core_copy(0, q).start()

    def left_group(q, carry):
        for g in range(J // G):
            gated(q * J + g * G, slice(0, 2 * C), left, True)
        return carry

    lax.fori_loop(0, chunks, left_group, 0)

    def dest_of(source, q):
        start = source * rows + q * J
        return start // cols, lax.rem(start, cols) // J

    at_end = jnp.logical_or(c == 0, c == N - 1)

    def send_slot(sent):
        slot = end_send.at[lax.rem(sent, DEPTH)]

        @pl.when(sent >= DEPTH)
        def _():
            sum_copy(inner, 0, slot).wait_send()

        return slot

    def block(source, q, sent):
        dest, p = dest_of(source, q)
        keep = jnp.logical_or(dest == c, adds_to(c, dest))
        for k in range(cols):
            right_k[k] = rights[source, q, k].astype(F32)

        def group(g, carry):
            totals = [jnp.zeros((J, C), F32)] * G
            for k in range(cols):
                factor = right_k[k]
                for i in range(G):
                    totals[i] += left[pl.ds((g * G + i) * cols + k, 1), :] * factor

            @pl.when(keep)
            def _():
                for i in range(G):
                    kept[dest, p, g * G + i] = totals[i]

            @pl.when(jnp.logical_not(keep))
            def _():
                for i in range(G):
                    outbox[dest, p, g * G + i] = totals[i].astype(BF16)

            return carry

        lax.fori_loop(0, rows // G, group, 0)

        @pl.when(jnp.logical_not(keep))
        def _():
            if N < 4:
                sum_copy(dest, p).start()
            else:

                @pl.when(jnp.logical_not(at_end))
                def _():
                    sum_copy(dest, p).start()

        if N < 4:
            return sent
        far = jnp.logical_and(at_end, passes_on(c, dest))
        near = jnp.logical_and(at_end, jnp.logical_and(dest == inner, p == 0))

        @pl.when(far)
        def _():
            pass_copy(dest, p, send_slot(sent)).start()

        @pl.when(near)
        def _():
            sum_copy(dest, p, send_slot(sent)).start()

        return sent + jnp.where(jnp.logical_or(far, near), 1, 0)

    def forward(source, q):
        dest, p = dest_of(source, q)

        @pl.when(adds_to(c, dest))
        def _():
            pass_arrival(dest, p).wait_recv()

            def group(g, carry):
                where = (dest, p, pl.ds(g * G, G))
                outbox[where] = (kept[where] + outbox[where].astype(F32)).astype(BF16)
                return carry

            lax.fori_loop(0, rows // G, group, 0)
            sum_copy(dest, p).start()

    sent = jnp.int32(0)
    for d in range(half):
        source = lax.rem(r + R - 2 * d, R)
        other = lax.rem(sibling + R - 2 * d, R)

        def mine(q, carry):
            if d > 0:
                right_arrival(source, q).wait_recv()
                core_copy(d, q).start()
            return block(source, q, carry)

        def siblings(q, carry):
            right_arrival(other, q).wait_recv()
            return block(other, q, carry)

        sent = lax.fori_loop(0, chunks, mine, sent)
        sent = lax.fori_loop(0, chunks, siblings, sent)

    if N >= 4:

        @pl.when(at_end)
        def _():
            for p in range(1, parts):
                sum_copy(inner, p, send_slot(sent + p - 1)).start()

    if N >= 4:
        for d in range(half):
            for source in (lax.rem(r + R - 2 * d, R), lax.rem(sibling + R - 2 * d, R)):

                def passed(q, carry):
                    forward(source, q)
                    return carry

                lax.fori_loop(0, chunks, passed, 0)

    def gate_group(g, carry):
        tokens = pl.ds(pl.multiple_of(g * G * cols, G * cols), G * cols)
        product = jnp.dot(normed[tokens, :], w_in_ref[:, 4 * C :], preferred_element_type=F32)
        out_ref[pl.ds(g * G, G)] = jax.nn.sigmoid(product).reshape(G, cols, C)
        return carry

    lax.fori_loop(0, rows // G, gate_group, 0)

    for load in loads[6:]:
        load.wait()

    if N < 4:
        sources = [lax.rem(c + d, N) for d in range(1, N)]
    else:
        ends = jnp.where(c == 1, 0, jnp.where(c == N - 2, N - 1, c))
        sources = [jnp.where(c == n, ends, n) for n in range(1, N - 1)]

    for p in range(parts):
        for source in sources:
            if N <= 4:
                sum_arrival(source, p).wait_recv()
            else:

                @pl.when(source != c)
                def _():
                    sum_arrival(source, p).wait_recv()

                    def collect(g, carry):
                        group = pl.ds(g * G, G)
                        kept[c, p, group] += inbox[source, p, group].astype(F32)
                        return carry

                    lax.fori_loop(0, rows // G, collect, 0)

        def final_group(g, carry):
            group = pl.ds(g * J, J)
            mixed = kept[c, p, group]
            if N <= 4:
                for source in sources:
                    mixed += inbox[source, p, group].astype(F32)
            mixed_norm = layer_norm(mixed.reshape(J * J, C), out_gain_ref[...], out_bias_ref[...])
            update = jnp.dot(mixed_norm.astype(BF16), w_out_ref[...], preferred_element_type=F32)
            where = (group, pl.ds(p * J, J))
            out_ref[where] = out_ref[where] * update.reshape(J, J, C)
            return carry

        lax.fori_loop(0, chunks, final_group, 0)

    for q in range(chunks):
        for d in range(half):
            if d > 0:
                direct_copy(d, q).wait_send()
            core_copy(d, q).wait_send()
    if N < 4:
        for d in range(1, N):
            for p in range(parts):
                sum_copy(lax.rem(c + d, N), p).wait_send()
    else:

        @pl.when(jnp.logical_not(at_end))
        def _():
            for d in range(1, N):
                for p in range(parts):
                    sum_copy(lax.rem(c + d, N), p).wait_send()

        @pl.when(at_end)
        def _():
            for n in range(DEPTH):
                slot = end_send.at[lax.rem(sent + parts - 1 + n, DEPTH)]
                sum_copy(inner, 0, slot).wait_send()


def solution(mesh):
    R, N = mesh.shape["row"], mesh.shape["col"]

    def per_device(
        pair_rep,
        chain_ids,
        residue_mask,
        norm_gain,
        norm_bias,
        chain_bias,
        proj_in,
        out_gain,
        out_bias,
        proj_out,
    ):
        rows, cols, _ = pair_rep.shape
        chunks, parts = rows // J, cols // J
        tokens = rows * cols
        dma = pltpu.SemaphoreType.DMA
        buffers = [
            pltpu.VMEM(pair_rep.shape, F32),
            pltpu.VMEM((1, chain_ids.shape[0]), jnp.int32),
            pltpu.VMEM((1, chain_ids.shape[0]), jnp.int32),
            pltpu.VMEM((1, C), F32),
            pltpu.VMEM((1, C), F32),
            pltpu.VMEM((1, C), F32),
            pltpu.VMEM(proj_in.shape, BF16),
            pltpu.VMEM((1, C), F32),
            pltpu.VMEM((1, C), F32),
            pltpu.VMEM(proj_out.shape, BF16),
            pltpu.VMEM((rows, C), F32),
            pltpu.VMEM((cols, C), F32),
            pltpu.VMEM((rows, C), F32),
            pltpu.VMEM((cols, C), F32),
            pltpu.VMEM((tokens, C), BF16),
            pltpu.VMEM((tokens, C), F32),
            pltpu.VMEM((tokens, C), F32),
            pltpu.VMEM((cols, J, C), F32),
            pltpu.VMEM((R, chunks, cols, J, C), BF16),
            pltpu.VMEM((N, parts, rows, J, C), F32),
            pltpu.VMEM((N, parts, rows, J, C), BF16),
            pltpu.VMEM((N, parts, rows, J, C), BF16),
        ]
        semaphores = [
            dma((9,)),
            dma((chunks,)),
            dma((R // 2, chunks)),
            dma((R // 2, chunks)),
            dma((R, chunks)),
            dma((N, parts)),
            dma((N, parts)),
            dma((N, parts)),
            dma((DEPTH,)),
        ]
        held = sum(math.prod(b.shape) * jnp.dtype(b.dtype).itemsize for b in buffers)
        update = pl.pallas_call(
            functools.partial(kernel, R, N),
            out_shape=jax.ShapeDtypeStruct(pair_rep.shape, F32),
            in_specs=[pl.BlockSpec(memory_space=pltpu.HBM)] * 10,
            out_specs=pl.BlockSpec(memory_space=pltpu.VMEM),
            scratch_shapes=buffers + semaphores,
            compiler_params=pltpu.CompilerParams(
                collective_id=0, has_side_effects=True, vmem_limit_bytes=max(held, 48 * 1024 * 1024) + 8 * 1024 * 1024
            ),
        )(
            pair_rep,
            chain_ids.reshape(1, -1),
            residue_mask.reshape(1, -1),
            norm_gain.reshape(1, C),
            norm_bias.reshape(1, C),
            chain_bias.reshape(1, C),
            proj_in,
            out_gain.reshape(1, C),
            out_bias.reshape(1, C),
            proj_out,
        )
        return pair_rep + update

    return jax.shard_map(
        per_device,
        mesh=mesh,
        in_specs=(
            P(("groups", "row"), "col", None),
            P("groups"),
            P("groups"),
            P(),
            P(),
            P(),
            P(),
            P(),
            P(),
            P(),
        ),
        out_specs=P(("groups", "row"), "col", None),
        check_vma=False,
    )
```

```python
import functools
import math

import jax
import jax.numpy as jnp
from jax import lax
from jax.experimental import pallas as pl
from jax.experimental.pallas import tpu as pltpu
from jax.sharding import PartitionSpec as P

C = 128
G = 8
J = 16
H = 2
DEPTH = 3
F32 = jnp.float32
BF16 = jnp.bfloat16


def layer_norm(values, gain, bias):
    center = values - jnp.mean(values, axis=-1, keepdims=True)
    variance = jnp.mean(center * center, axis=-1, keepdims=True)
    return center * lax.rsqrt(variance + 1e-05) * gain + bias


def as_rows(ref, offset, count):
    shape = (count, ref.shape[1])
    lane = lax.broadcasted_iota(jnp.int32, shape, 1)
    row = lax.broadcasted_iota(jnp.int32, shape, 0)
    values = jnp.broadcast_to(ref[...].astype(F32), shape)
    picked = jnp.sum(jnp.where(lane == row + offset, values, 0.0), axis=1, keepdims=True)
    return jnp.broadcast_to(picked, (count, C))


def kernel(
    R,
    N,
    pair_hbm,
    chain_hbm,
    mask_hbm,
    gain_hbm,
    bias_hbm,
    chain_bias_hbm,
    w_in_hbm,
    out_gain_hbm,
    out_bias_hbm,
    w_out_hbm,
    out_ref,
    pair_ref,
    chain_ref,
    mask_ref,
    gain_ref,
    bias_ref,
    chain_bias_ref,
    w_in_ref,
    out_gain_ref,
    out_bias_ref,
    w_out_ref,
    row_chain,
    col_chain,
    row_live,
    col_live,
    normed,
    left,
    right,
    right_k,
    rights,
    kept,
    outbox,
    inbox,
    load_sem,
    pair_sem,
    direct_send,
    core_send,
    right_recv,
    sum_send,
    sum_recv,
    pass_recv,
    end_send,
):
    rows, cols, _ = pair_ref.shape
    chunks = rows // J
    parts = cols // J
    pieces = parts * H
    tall = rows // H
    r = lax.axis_index("row")
    c = lax.axis_index("col")
    sibling = r + 1 - 2 * lax.rem(r, 2)
    half = R // 2

    smalls = [
        (chain_hbm, chain_ref),
        (mask_hbm, mask_ref),
        (gain_hbm, gain_ref),
        (bias_hbm, bias_ref),
        (chain_bias_hbm, chain_bias_ref),
        (w_in_hbm, w_in_ref),
        (out_gain_hbm, out_gain_ref),
        (out_bias_hbm, out_bias_ref),
        (w_out_hbm, w_out_ref),
    ]
    loads = [
        pltpu.make_async_copy(src, dst, load_sem.at[n]) for n, (src, dst) in enumerate(smalls)
    ]
    pair_loads = [
        pltpu.make_async_copy(
            pair_hbm.at[pl.ds(q * J, J)], pair_ref.at[pl.ds(q * J, J)], pair_sem.at[q]
        )
        for q in range(chunks)
    ]
    for load in loads[:2] + pair_loads[:1] + loads[2:] + pair_loads[1:]:
        load.start()

    barrier = pltpu.get_barrier_semaphore()
    pl.semaphore_signal(barrier, inc=1, device_id={"row": sibling})
    for d in range(1, half):
        pl.semaphore_signal(barrier, inc=1, device_id={"row": lax.rem(r + 2 * d, R)})
    for d in range(1, N):
        pl.semaphore_signal(barrier, inc=1, device_id={"col": lax.rem(c + d, N)})

    for load in loads[:2]:
        load.wait()
    row_chain[...] = as_rows(chain_ref, r * rows, rows)
    col_chain[...] = as_rows(chain_ref, c * cols, cols)
    row_live[...] = as_rows(mask_ref, r * rows, rows)
    col_live[...] = as_rows(mask_ref, c * cols, cols)

    def direct_copy(d, q):
        return pltpu.make_async_remote_copy(
            src_ref=rights.at[r, q],
            dst_ref=rights.at[r, q],
            send_sem=direct_send.at[d, q],
            recv_sem=right_recv.at[r, q],
            device_id={"row": lax.rem(r + 2 * d, R)},
        )

    def core_copy(d, q):
        source = lax.rem(r + R - 2 * d, R)
        return pltpu.make_async_remote_copy(
            src_ref=rights.at[source, q],
            dst_ref=rights.at[source, q],
            send_sem=core_send.at[d, q],
            recv_sem=right_recv.at[source, q],
            device_id={"row": sibling},
        )

    def right_arrival(source, q):
        return pltpu.make_async_remote_copy(
            src_ref=rights.at[source, q],
            dst_ref=rights.at[source, q],
            send_sem=core_send.at[0, q],
            recv_sem=right_recv.at[source, q],
            device_id={"row": sibling},
        )

    def passes_on(device, dest):
        if N < 4:
            return False
        low = jnp.logical_and(device == 0, dest >= 2)
        return jnp.logical_or(low, jnp.logical_and(device == N - 1, dest <= N - 3))

    def adds_to(device, dest):
        if N < 4:
            return False
        low = jnp.logical_and(device == 1, dest >= 2)
        return jnp.logical_or(low, jnp.logical_and(device == N - 2, dest <= N - 3))

    inner = jnp.where(c == 0, 1, N - 2)
    outer = jnp.where(c == 1, 0, N - 1)

    def pass_copy(dest, p, send_sem):
        return pltpu.make_async_remote_copy(
            src_ref=outbox.at[dest, p],
            dst_ref=outbox.at[dest, p],
            send_sem=send_sem,
            recv_sem=pass_recv.at[dest, p],
            device_id={"col": inner},
        )

    def pass_arrival(dest, p):
        return pltpu.make_async_remote_copy(
            src_ref=outbox.at[dest, p],
            dst_ref=outbox.at[dest, p],
            send_sem=sum_send.at[dest, p],
            recv_sem=pass_recv.at[dest, p],
            device_id={"col": outer},
        )

    def sum_copy(dest, p, send_sem=None):
        return pltpu.make_async_remote_copy(
            src_ref=outbox.at[dest, p],
            dst_ref=inbox.at[c, p],
            send_sem=sum_send.at[dest, p] if send_sem is None else send_sem,
            recv_sem=sum_recv.at[c, p],
            device_id={"col": dest},
        )

    def sum_arrival(source, p):
        return pltpu.make_async_remote_copy(
            src_ref=outbox.at[source, p],
            dst_ref=inbox.at[source, p],
            send_sem=sum_send.at[source, p],
            recv_sem=sum_recv.at[source, p],
            device_id={"col": source},
        )

    def gated(base, columns, target, rounded):
        tokens = pl.ds(pl.multiple_of(base * cols, G * cols), G * cols)
        product = jnp.dot(normed[tokens, :], w_in_ref[:, columns], preferred_element_type=F32)
        for i in range(G):
            block = product[i * cols : (i + 1) * cols]
            mask = row_live[pl.ds(base + i, 1), :] * col_live[...]
            value = jax.nn.sigmoid(block[:, :C]) * block[:, C:] * mask
            if rounded:
                value = value.astype(BF16).astype(F32)
            target[pl.ds(pl.multiple_of((base + i) * cols, cols), cols), :] = value

    def right_group(base):
        for i in range(J):
            same = row_chain[pl.ds(base + i, 1), :] == col_chain[...]
            pair_in = pair_ref[base + i] + jnp.where(same, chain_bias_ref[...], 0.0)
            tokens = pl.ds(pl.multiple_of((base + i) * cols, cols), cols)
            normed[tokens, :] = layer_norm(pair_in, gain_ref[...], bias_ref[...]).astype(BF16)
        for g in range(J // G):
            gated(base + g * G, slice(2 * C, 4 * C), right, False)

    for q in range(chunks):
        if q == 0:
            for load in loads[2:6]:
                load.wait()
        pair_loads[q].wait()
        right_group(q * J)
        for k in range(cols):
            rights[r, q, k] = right[pl.ds(q * J * cols + k, J, stride=cols), :].astype(BF16)
        if q == 0:
            pl.semaphore_wait(barrier, 1 + (half - 1) + (N - 1))
        for d in range(1, half):
            direct_copy(d, q).start()
        core_copy(0, q).start()

    def left_group(q, carry):
        for g in range(J // G):
            gated(q * J + g * G, slice(0, 2 * C), left, True)
        return carry

    lax.fori_loop(0, chunks, left_group, 0)

    def dest_of(source, q):
        start = source * rows + q * J
        return start // cols, lax.rem(start, cols) // J

    at_end = jnp.logical_or(c == 0, c == N - 1)

    def send_slot(sent):
        slot = end_send.at[lax.rem(sent, DEPTH)]

        @pl.when(sent >= DEPTH)
        def _():
            sum_copy(inner, 0, slot).wait_send()

        return slot

    def block(source, q, sent):
        dest, p = dest_of(source, q)
        keep = jnp.logical_or(dest == c, adds_to(c, dest))
        for k in range(cols):
            right_k[k] = rights[source, q, k].astype(F32)

        for h in range(H):
            piece = p * H + h

            def group(g, carry):
                totals = [jnp.zeros((J, C), F32)] * G
                for k in range(cols):
                    factor = right_k[k]
                    for i in range(G):
                        row = h * tall + g * G + i
                        totals[i] += left[pl.ds(row * cols + k, 1), :] * factor

                @pl.when(keep)
                def _():
                    for i in range(G):
                        kept[dest, piece, g * G + i] = totals[i]

                @pl.when(jnp.logical_not(keep))
                def _():
                    for i in range(G):
                        outbox[dest, piece, g * G + i] = totals[i].astype(BF16)

                return carry

            lax.fori_loop(0, tall // G, group, 0)

            @pl.when(jnp.logical_not(keep))
            def _():
                if N < 4:
                    sum_copy(dest, piece).start()
                else:

                    @pl.when(jnp.logical_not(at_end))
                    def _():
                        sum_copy(dest, piece).start()

            if N >= 4:
                far = jnp.logical_and(at_end, passes_on(c, dest))
                near = jnp.logical_and(at_end, jnp.logical_and(dest == inner, p == 0))

                @pl.when(far)
                def _():
                    pass_copy(dest, piece, send_slot(sent)).start()

                @pl.when(near)
                def _():
                    sum_copy(dest, piece, send_slot(sent)).start()

                sent = sent + jnp.where(jnp.logical_or(far, near), 1, 0)
        return sent

    def forward(source, q):
        dest, p = dest_of(source, q)

        @pl.when(adds_to(c, dest))
        def _():
            for h in range(H):
                piece = p * H + h
                pass_arrival(dest, piece).wait_recv()
                for g in range(tall // G):
                    where = (dest, piece, pl.ds(g * G, G))
                    outbox[where] = (kept[where] + outbox[where].astype(F32)).astype(BF16)
                sum_copy(dest, piece).start()

    sent = jnp.int32(0)
    for d in range(half):
        source = lax.rem(r + R - 2 * d, R)
        other = lax.rem(sibling + R - 2 * d, R)

        def mine(q, carry):
            if d > 0:
                right_arrival(source, q).wait_recv()
                core_copy(d, q).start()
            return block(source, q, carry)

        def siblings(q, carry):
            right_arrival(other, q).wait_recv()
            return block(other, q, carry)

        sent = lax.fori_loop(0, chunks, mine, sent)
        sent = lax.fori_loop(0, chunks, siblings, sent)

    if N >= 4:

        @pl.when(at_end)
        def _():
            for n in range(H, pieces):
                sum_copy(inner, n, send_slot(sent + n - H)).start()

    if N >= 4:
        for d in range(half):
            for source in (lax.rem(r + R - 2 * d, R), lax.rem(sibling + R - 2 * d, R)):

                def passed(q, carry):
                    forward(source, q)
                    return carry

                lax.fori_loop(0, chunks, passed, 0)

    def gate_group(g, carry):
        tokens = pl.ds(pl.multiple_of(g * G * cols, G * cols), G * cols)
        product = jnp.dot(normed[tokens, :], w_in_ref[:, 4 * C :], preferred_element_type=F32)
        out_ref[pl.ds(g * G, G)] = jax.nn.sigmoid(product).reshape(G, cols, C)
        return carry

    lax.fori_loop(0, rows // G, gate_group, 0)

    for load in loads[6:]:
        load.wait()

    if N < 4:
        sources = [lax.rem(c + d, N) for d in range(1, N)]
    else:
        ends = jnp.where(c == 1, 0, jnp.where(c == N - 2, N - 1, c))
        sources = [jnp.where(c == n, ends, n) for n in range(1, N - 1)]

    for piece in range(pieces):
        p, h = piece // H, piece % H
        for source in sources:
            if N <= 4:
                sum_arrival(source, piece).wait_recv()
            else:

                @pl.when(source != c)
                def _():
                    sum_arrival(source, piece).wait_recv()

                    def collect(g, carry):
                        group = pl.ds(g * G, G)
                        kept[c, piece, group] += inbox[source, piece, group].astype(F32)
                        return carry

                    lax.fori_loop(0, tall // G, collect, 0)

        def final_group(g, carry):
            group = pl.ds(g * J, J)
            mixed = kept[c, piece, group]
            if N <= 4:
                for source in sources:
                    mixed += inbox[source, piece, group].astype(F32)
            mixed_norm = layer_norm(mixed.reshape(J * J, C), out_gain_ref[...], out_bias_ref[...])
            update = jnp.dot(mixed_norm.astype(BF16), w_out_ref[...], preferred_element_type=F32)
            where = (pl.ds(h * tall + g * J, J), pl.ds(p * J, J))
            out_ref[where] = out_ref[where] * update.reshape(J, J, C)
            return carry

        lax.fori_loop(0, tall // J, final_group, 0)

    for q in range(chunks):
        for d in range(half):
            if d > 0:
                direct_copy(d, q).wait_send()
            core_copy(d, q).wait_send()
    if N < 4:
        for d in range(1, N):
            for piece in range(pieces):
                sum_copy(lax.rem(c + d, N), piece).wait_send()
    else:

        @pl.when(jnp.logical_not(at_end))
        def _():
            for d in range(1, N):
                for piece in range(pieces):
                    sum_copy(lax.rem(c + d, N), piece).wait_send()

        @pl.when(at_end)
        def _():
            for n in range(DEPTH):
                slot = end_send.at[lax.rem(sent + pieces - H + n, DEPTH)]
                sum_copy(inner, 0, slot).wait_send()


def solution(mesh):
    R, N = mesh.shape["row"], mesh.shape["col"]

    def per_device(
        pair_rep,
        chain_ids,
        residue_mask,
        norm_gain,
        norm_bias,
        chain_bias,
        proj_in,
        out_gain,
        out_bias,
        proj_out,
    ):
        rows, cols, _ = pair_rep.shape
        chunks, parts = rows // J, cols // J
        tokens = rows * cols
        dma = pltpu.SemaphoreType.DMA
        buffers = [
            pltpu.VMEM(pair_rep.shape, F32),
            pltpu.VMEM((1, chain_ids.shape[0]), jnp.int32),
            pltpu.VMEM((1, chain_ids.shape[0]), jnp.int32),
            pltpu.VMEM((1, C), F32),
            pltpu.VMEM((1, C), F32),
            pltpu.VMEM((1, C), F32),
            pltpu.VMEM(proj_in.shape, BF16),
            pltpu.VMEM((1, C), F32),
            pltpu.VMEM((1, C), F32),
            pltpu.VMEM(proj_out.shape, BF16),
            pltpu.VMEM((rows, C), F32),
            pltpu.VMEM((cols, C), F32),
            pltpu.VMEM((rows, C), F32),
            pltpu.VMEM((cols, C), F32),
            pltpu.VMEM((tokens, C), BF16),
            pltpu.VMEM((tokens, C), F32),
            pltpu.VMEM((tokens, C), F32),
            pltpu.VMEM((cols, J, C), F32),
            pltpu.VMEM((R, chunks, cols, J, C), BF16),
            pltpu.VMEM((N, parts * H, rows // H, J, C), F32),
            pltpu.VMEM((N, parts * H, rows // H, J, C), BF16),
            pltpu.VMEM((N, parts * H, rows // H, J, C), BF16),
        ]
        semaphores = [
            dma((9,)),
            dma((chunks,)),
            dma((R // 2, chunks)),
            dma((R // 2, chunks)),
            dma((R, chunks)),
            dma((N, parts * H)),
            dma((N, parts * H)),
            dma((N, parts * H)),
            dma((DEPTH,)),
        ]
        held = sum(math.prod(b.shape) * jnp.dtype(b.dtype).itemsize for b in buffers)
        update = pl.pallas_call(
            functools.partial(kernel, R, N),
            out_shape=jax.ShapeDtypeStruct(pair_rep.shape, F32),
            in_specs=[pl.BlockSpec(memory_space=pltpu.HBM)] * 10,
            out_specs=pl.BlockSpec(memory_space=pltpu.VMEM),
            scratch_shapes=buffers + semaphores,
            compiler_params=pltpu.CompilerParams(
                collective_id=0, has_side_effects=True, vmem_limit_bytes=max(held, 48 * 1024 * 1024) + 8 * 1024 * 1024
            ),
        )(
            pair_rep,
            chain_ids.reshape(1, -1),
            residue_mask.reshape(1, -1),
            norm_gain.reshape(1, C),
            norm_bias.reshape(1, C),
            chain_bias.reshape(1, C),
            proj_in,
            out_gain.reshape(1, C),
            out_bias.reshape(1, C),
            proj_out,
        )
        return pair_rep + update

    return jax.shard_map(
        per_device,
        mesh=mesh,
        in_specs=(
            P(("groups", "row"), "col", None),
            P("groups"),
            P("groups"),
            P(),
            P(),
            P(),
            P(),
            P(),
            P(),
            P(),
        ),
        out_specs=P(("groups", "row"), "col", None),
        check_vma=False,
    )
```
